512 devices in a mesh: dp: 16 (over z_lo, core), latent: 32 (over y, x, z_hi).
Axes of the slice: x: 4, y: 4, z: 16 (z_hi: 2, z_lo: 8; z = z_hi * 8 + z_lo), core: 2. Of those that a mesh axis runs over, the one named last changes fastest.
Arguments:
- activations: bfloat16 [3072, 4608], P('dp', 'latent'), may hold values from -16 to 16
- encoder: float32 [4608, 8192], P('dp', 'latent'), may hold values from -0.09375 to 0.09375
- enc_bias: float32 [8192], P('latent'), may hold values from -3 to 3
- decoder: float32 [4608, 8192], P('dp', 'latent'), may hold values from -5 to 5
- enc_moment: float32 [4608, 8192], P('dp', 'latent'), may hold values from -0.3 to 0.3
- enc_second: float32 [4608, 8192], P('dp', 'latent'), may hold values from 2.6041667e-05 to 0.00026041668
- bias_moment: float32 [8192], P('latent'), may hold values from -3 to 3
- bias_second: float32 [8192], P('latent'), may hold values from 0.001 to 0.01
- dec_moment: float32 [4608, 8192], P('dp', 'latent'), may hold values from -0.48 to 0.48
- dec_second: float32 [4608, 8192], P('dp', 'latent'), may hold values from 1.6276043e-05 to 0.00016276042
Outputs:
- enc_update: float32 [4608, 8192], P('dp', 'latent')
- bias_update: float32 [8192], P('latent')
- dec_update: float32 [4608, 8192], P('dp', 'latent')
The draws below stay inside these ranges and needn't reach their ends.
All inputs are finite; a program needn't handle non-finite values.
Results may differ from the reference program's by a relative error of at most 0.035.
The reference program's roundings to bfloat16 on the way (of `enc_weights`, `dec_weights`, `codes`, `error` and `back`) count: a program that leaves them out, or rounds other values in their place, can miss the bound.
Values may be sent and summed in bfloat16 or wider, within the bound.
No kernel may reach another device: no remote copies, remote signals or barrier semaphores. Data moves between devices by JAX's collectives and lax.ppermute only.
A program may use at most 64 MiB of HBM per device.

```python
import math
import jax
import jax.numpy as jnp
from jax import lax

D = 4608
LAT_DEV = 256
LATENTS = 8192
TOK_DEV = 192
TOKENS = 3072


def draw_activations(key, part):
    key = jax.random.fold_in(key, 11)
    base_key = jax.random.fold_in(key, 0)
    position = jnp.arange(TOKENS, dtype=jnp.float32) / TOKENS
    base = jnp.clip(jax.random.normal(base_key, (TOKENS, D), jnp.float32), -5.0, 5.0)
    scale = jnp.exp(math.log(10.0) * (position - 0.5))
    return (base * scale[:, None]).astype(jnp.bfloat16)


def draw_decoder(key, part):
    key = jax.random.fold_in(key, 23)
    entry_key, latent_key = jax.random.split(key)
    position = jnp.arange(D, dtype=jnp.float32) / D
    entries = jnp.clip(jax.random.normal(entry_key, (D, LATENTS), jnp.float32), -5.0, 5.0)
    column = jnp.exp(math.log(10.0) * (position - 0.5))
    latent = jnp.exp(jax.random.uniform(latent_key, (LATENTS,), jnp.float32, math.log(0.3), math.log(3.0)))
    return entries * column[:, None] * latent[None, :] / math.sqrt(LATENTS)


def shard_levels(key, shape, cuts, smallest, high):
    gain, own = 1.0, jax.random.fold_in(key, 6)
    for dim, parts in cuts:
        steps = jnp.exp(jax.random.uniform(jax.random.fold_in(own, dim), (parts,), jnp.float32, smallest / len(cuts), high / len(cuts)))
        gain = gain * jnp.repeat(steps, shape[dim] // parts).reshape([-1 if axis == dim else 1 for axis in range(len(shape))])
    return gain


def normal_values(own_key, extent, scale, most, pieces=(), kind=jnp.bfloat16):
    gain = shard_levels(own_key, extent, pieces, -0.22, 0.18) if pieces else 1.0
    drawn = jax.random.normal(own_key, extent, jnp.float32) * scale * gain
    return jnp.minimum(jnp.maximum(drawn, -most), most).astype(kind)


def setup_inputs(seed: int = 0) -> dict:
    key_list = jax.random.split(jax.random.key(seed), 11)
    activations = draw_activations(jax.random.fold_in(key_list[10], 71), 0)
    encoder = normal_values(key_list[1], (D, LATENTS), D ** -0.5, 0.09375, ((0, 16), (1, 32)), jnp.float32)
    enc_bias = normal_values(key_list[2], (LATENTS,), 0.5, 3.0, ((0, 32),), jnp.float32)
    decoder = draw_decoder(jax.random.fold_in(key_list[10], 71), 0)
    enc_moment = normal_values(key_list[4], (D, LATENTS), 0.05, 0.3, ((0, 16), (1, 32)), jnp.float32)
    enc_second = jnp.clip(jnp.exp(math.log(0.00026041668) - 2.3025851 * jax.random.uniform(key_list[5], (D, LATENTS), jnp.float32) ** shard_levels(key_list[5], (D, LATENTS), ((0, 16), (1, 32)), -0.2, 0.2)), 2.604166729724966e-05, 0.00026041668)
    bias_moment = normal_values(key_list[6], (LATENTS,), 0.5, 3.0, ((0, 32),), jnp.float32)
    bias_second = jnp.clip(jnp.exp(math.log(0.01) - 2.30258502 * jax.random.uniform(key_list[7], (LATENTS,), jnp.float32) ** shard_levels(key_list[7], (LATENTS,), ((0, 32),), -0.2, 0.2)), 0.001, 0.01)
    dec_moment = normal_values(key_list[8], (D, LATENTS), 0.08, 0.48, ((0, 16), (1, 32)), jnp.float32)
    dec_second = jnp.clip(jnp.exp(math.log(0.00016276042) - 2.3025851 * jax.random.uniform(key_list[9], (D, LATENTS), jnp.float32) ** shard_levels(key_list[9], (D, LATENTS), ((0, 16), (1, 32)), -0.2, 0.2)), 1.627604251552839e-05, 0.00016276042)
    return dict(activations=activations, encoder=encoder, enc_bias=enc_bias, decoder=decoder, enc_moment=enc_moment, enc_second=enc_second, bias_moment=bias_moment, bias_second=bias_second, dec_moment=dec_moment, dec_second=dec_second)


penalty = 3.0
beta_one = 0.9
beta_two = 0.999
step_count = 10.0
tiny_eps = 1e-08
norm_eps = 1e-06

def rounded(values):
    return lax.optimization_barrier(values.astype(jnp.bfloat16)).astype(jnp.float32)

def adam_update(grad, moment, second):
    first_new = beta_one * moment + (1.0 - beta_one) * grad
    second_new = beta_two * second + (1.0 - beta_two) * grad * grad
    first_hat = first_new / (1.0 - beta_one ** step_count)
    second_hat = second_new / (1.0 - beta_two ** step_count)
    return first_hat / (jnp.sqrt(second_hat) + tiny_eps)

def reference(activations, encoder, enc_bias, decoder, enc_moment, enc_second, bias_moment, bias_second, dec_moment, dec_second):
    enc_weights = encoder.astype(jnp.bfloat16)
    dec_weights = decoder.astype(jnp.bfloat16)
    norms = jnp.sqrt(lax.optimization_barrier(jnp.sum(jnp.square(dec_weights.astype(jnp.float32)), axis=0)) + norm_eps)
    pre = jnp.dot(activations, enc_weights, preferred_element_type=jnp.float32) + enc_bias[None, :]
    codes = jnp.maximum(pre, 0.0).astype(jnp.bfloat16)

    def add_block(total, index):
        start = (index * LAT_DEV).astype(jnp.int32)
        block_codes = lax.dynamic_slice_in_dim(codes, start, LAT_DEV, 1)
        block_weights = lax.dynamic_slice_in_dim(dec_weights, start, LAT_DEV, 1)
        part = jnp.dot(block_codes, block_weights.T, preferred_element_type=jnp.float32)
        return (total + rounded(part), None)
    recon, unused = lax.scan(add_block, jnp.zeros((TOKENS, D), jnp.float32), jnp.arange(LATENTS // LAT_DEV, dtype=jnp.int32))
    error = (recon - activations.astype(jnp.float32)).astype(jnp.bfloat16)
    dcodes = 2.0 / TOKENS * jnp.dot(error, dec_weights, preferred_element_type=jnp.float32) + penalty / TOKENS * norms[None, :]
    back = jnp.where(pre > 0.0, dcodes, 0.0).astype(jnp.bfloat16)

    def add_rows(totals, index):
        start = (index * TOK_DEV).astype(jnp.int32)
        rows = lax.dynamic_slice_in_dim(activations, start, TOK_DEV, 0)
        grad_rows = lax.dynamic_slice_in_dim(back, start, TOK_DEV, 0)
        error_rows = lax.dynamic_slice_in_dim(error, start, TOK_DEV, 0)
        code_rows = lax.dynamic_slice_in_dim(codes, start, TOK_DEV, 0)
        enc_part = jnp.dot(rows.T, grad_rows, preferred_element_type=jnp.float32)
        dec_part = 2.0 / TOKENS * jnp.dot(error_rows.T, code_rows, preferred_element_type=jnp.float32)
        return ((totals[0] + rounded(enc_part), totals[1] + rounded(dec_part)), None)
    zeros_both = (jnp.zeros((D, LATENTS), jnp.float32), jnp.zeros((D, LATENTS), jnp.float32))
    grads, unused = lax.scan(add_rows, zeros_both, jnp.arange(TOKENS // TOK_DEV, dtype=jnp.int32))
    enc_grad, data_grad = grads
    bias_grad = lax.optimization_barrier(jnp.sum(back.astype(jnp.float32), axis=0))
    usage = lax.optimization_barrier(jnp.sum(codes.astype(jnp.float32), axis=0))
    dec_grad = data_grad + penalty * (usage / TOKENS)[None, :] * decoder / norms[None, :]
    enc_update = adam_update(enc_grad, enc_moment, enc_second)
    bias_update = adam_update(bias_grad, bias_moment, bias_second)
    dec_update = adam_update(dec_grad, dec_moment, dec_second)
    return (enc_update, bias_update, dec_update)
```

```python
import jax
import jax.numpy as jnp
from jax import lax
from jax.sharding import Mesh, PartitionSpec as P

penalty = 3.0
beta_one = 0.9
beta_two = 0.999
step_count = 10.0
tiny_eps = 1e-08
norm_eps = 1e-06

names = ("zb", "zc", "zd", "core", "y1", "y0", "x1", "x0", "h")
depth_axes = ("zc", "zd")
plane_axes = ("y1", "y0", "x1", "x0")
row_axes = ("h", "zb", "core")
swap = ((0, 1), (1, 0))


def exchange(values, axes):
    return lax.all_to_all(values, axes, 0, 0, tiled=True)


def spread(values, axes):
    count = 1
    for axis in axes:
        count *= lax.axis_size(axis)
    copies = jnp.broadcast_to(values[None], (count,) + values.shape)
    return exchange(copies, axes).reshape((count * values.shape[0],) + values.shape[1:])


def total_over(values, axes):
    for axis in axes:
        values = values + lax.ppermute(values, axis, swap)
    return values


def add_blocks(values, axes):
    return jnp.sum(exchange(values, axes).astype(jnp.float32), axis=0)


def adam_update(grad, moment, second):
    first_new = beta_one * moment + (1.0 - beta_one) * grad
    second_new = beta_two * second + (1.0 - beta_two) * grad * grad
    first_hat = first_new / (1.0 - beta_one**step_count)
    second_hat = second_new / (1.0 - beta_two**step_count)
    return first_hat / (jnp.sqrt(second_hat) + tiny_eps)


def gather_weights(block):
    rows, columns = block.shape
    parts = lax.all_gather(block, row_axes, axis=0, tiled=False)
    parts = parts.reshape(2, 4 * rows, columns)
    return jnp.concatenate([parts[0], parts[1]], axis=1)


def scatter_grad(grad, rows, columns):
    blocks = grad.astype(jnp.bfloat16).reshape(4 * rows, 2, columns).transpose(1, 0, 2)
    return lax.psum_scatter(
        blocks.reshape(8 * rows, columns), row_axes, scatter_dimension=0, tiled=True
    ).astype(jnp.float32)


def body(
    activations,
    encoder,
    enc_bias,
    decoder,
    enc_moment,
    enc_second,
    bias_moment,
    bias_second,
    dec_moment,
    dec_second,
):
    rows_local, features = activations.shape
    total_rows = rows_local * 16
    depth, latents = encoder.shape
    enc_weights = gather_weights(encoder.astype(jnp.bfloat16))
    dec_weights = gather_weights(decoder.astype(jnp.bfloat16))
    half = lax.axis_index("h")
    other_bias = lax.ppermute(enc_bias, "h", swap)
    bias = jnp.where(
        half == 0, jnp.concatenate([enc_bias, other_bias]), jnp.concatenate([other_bias, enc_bias])
    )

    piece = rows_local // 32
    planes = exchange(activations.reshape(16, 2 * piece, features), plane_axes)
    planes = planes.reshape(2, 2, 2, 2, 2, piece, features)
    planes = planes.transpose(4, 1, 2, 5, 0, 3, 6).reshape(8, piece, 4, features)
    own = exchange(planes, ("h", "zc", "zd")).reshape(2, 4, piece, 4, features)
    own = own.transpose(1, 2, 3, 0, 4).reshape(4 * piece, 8 * features)
    acts = spread(own, plane_axes)
    rows = acts.shape[0]

    pre_part = jnp.dot(acts, enc_weights, preferred_element_type=jnp.float32)
    pre = add_blocks(pre_part.reshape(4, rows // 4, 2 * latents), depth_axes) + bias[None, :]
    codes = spread(jnp.maximum(pre, 0.0).astype(jnp.bfloat16), depth_axes)
    usage = total_over(jnp.sum(codes.astype(jnp.float32), axis=0), row_axes)
    squares = jnp.sum(jnp.square(dec_weights.astype(jnp.float32)), axis=0)
    norms = jnp.sqrt(total_over(squares, depth_axes) + norm_eps)

    recon_part = lax.dot_general(
        codes, dec_weights, (((1,), (1,)), ((), ())), preferred_element_type=jnp.float32
    ).astype(jnp.bfloat16)
    recon = add_blocks(recon_part.reshape(16, rows // 16, 4 * depth), plane_axes)
    error = spread((recon - own.astype(jnp.float32)).astype(jnp.bfloat16), plane_axes)

    back_part = jnp.dot(error, dec_weights, preferred_element_type=jnp.float32).astype(jnp.bfloat16)
    dcodes = (
        2.0 / total_rows * add_blocks(back_part.reshape(4, rows // 4, 2 * latents), depth_axes)
        + penalty / total_rows * norms[None, :]
    )
    back = spread(jnp.where(pre > 0.0, dcodes, 0.0).astype(jnp.bfloat16), depth_axes)
    bias_grad = total_over(jnp.sum(back.astype(jnp.float32), axis=0), row_axes)

    data_part = (
        2.0
        / total_rows
        * lax.dot_general(error, codes, (((0,), (0,)), ((), ())), preferred_element_type=jnp.float32)
    )
    data_grad = scatter_grad(data_part, depth, latents)
    enc_part = lax.dot_general(
        acts, back, (((0,), (0,)), ((), ())), preferred_element_type=jnp.float32
    )
    enc_grad = scatter_grad(enc_part, depth, latents)

    def own_latents(values):
        return jnp.where(half == 0, values[:latents], values[latents:])

    usage, bias_grad, norms = own_latents(usage), own_latents(bias_grad), own_latents(norms)
    dec_grad = data_grad + penalty * (usage / total_rows)[None, :] * decoder / norms[None, :]
    enc_update = adam_update(enc_grad, enc_moment, enc_second)
    bias_update = adam_update(bias_grad, bias_moment, bias_second)
    dec_update = adam_update(dec_grad, dec_moment, dec_second)
    return (enc_update, bias_update, dec_update)


def solution(mesh):
    fine = Mesh(mesh.devices.reshape((2,) * 9), names)
    dp, latent = names[:4], names[4:]
    matrix, vector = P(dp, latent), P(latent)
    in_specs = (matrix, matrix, vector, matrix, matrix, matrix, vector, vector, matrix, matrix)
    out_specs = (matrix, vector, matrix)
    return jax.shard_map(body, mesh=fine, in_specs=in_specs, out_specs=out_specs, check_vma=False)
```

```python
import jax
import jax.numpy as jnp
from jax import lax
from jax.sharding import Mesh, PartitionSpec as P

penalty = 3.0
beta_one = 0.9
beta_two = 0.999
step_count = 10.0
tiny_eps = 1e-08
norm_eps = 1e-06

names = ("zb", "zc", "zd", "core", "y1", "y0", "x1", "x0", "h")
depth_axes = ("zc", "zd")
plane_axes = ("y1", "y0", "x1", "x0")
row_axes = ("h", "zb")
swap = ((0, 1), (1, 0))
cross = ((0, 3), (1, 2), (2, 1), (3, 0))


def exchange(values, axes):
    return lax.all_to_all(values, axes, 0, 0, tiled=True)


def spread(values, axes):
    count = 1
    for axis in axes:
        count *= lax.axis_size(axis)
    copies = jnp.broadcast_to(values[None], (count,) + values.shape)
    return exchange(copies, axes).reshape((count * values.shape[0],) + values.shape[1:])


def spread_depth(values):
    place = 2 * lax.axis_index("zc") + lax.axis_index("zd")
    whole = jnp.zeros((4,) + values.shape, values.dtype)
    parts = (
        values,
        lax.ppermute(values, "zd", swap),
        lax.ppermute(values, "zc", swap),
        lax.ppermute(values, depth_axes, cross),
    )
    for offset, part in enumerate(parts):
        whole = lax.dynamic_update_index_in_dim(whole, part, place ^ offset, 0)
    return whole.reshape((4 * values.shape[0],) + values.shape[1:])


def total_over(values, axes):
    for axis in axes:
        values = values + lax.ppermute(values, axis, swap)
    return values


def add_blocks(values, axes):
    return jnp.sum(exchange(values, axes).astype(jnp.float32), axis=0)


def adam_update(grad, moment, second):
    first_new = beta_one * moment + (1.0 - beta_one) * grad
    second_new = beta_two * second + (1.0 - beta_two) * grad * grad
    first_hat = first_new / (1.0 - beta_one**step_count)
    second_hat = second_new / (1.0 - beta_two**step_count)
    return first_hat / (jnp.sqrt(second_hat) + tiny_eps)


def gather_weights(*blocks):
    count, (rows, columns) = len(blocks), blocks[0].shape
    parts = lax.all_gather(jnp.concatenate(blocks), row_axes + ("core",), axis=0, tiled=False)
    parts = parts.reshape(2, 4, count, rows, columns)
    parts = [[parts[half, :, index].reshape(4 * rows, columns) for half in range(2)] for index in range(count)]
    return [jnp.concatenate(halves, axis=1) for halves in parts]


def split_rows(values):
    high = values.astype(jnp.bfloat16)
    low = (values - high.astype(jnp.float32)).astype(jnp.bfloat16)
    padding = jnp.zeros((16 - 2 * values.shape[0],) + values.shape[1:], jnp.bfloat16)
    return jnp.concatenate([high, low, padding], 0)


def join_rows(rows, count):
    rows = rows.astype(jnp.float32)
    return rows[..., :count, :] + rows[..., count : 2 * count, :]


def core_blocks(grad, sums, rows, columns):
    core = lax.axis_index("core")
    grad = grad.reshape(2, 2, rows, 2 * columns)
    kept = lax.dynamic_index_in_dim(grad, core, 1, False).reshape(2 * rows, 2 * columns)
    given = lax.dynamic_index_in_dim(grad, 1 - core, 1, False).reshape(2 * rows, 2 * columns)
    given = given.astype(jnp.bfloat16)
    if sums is not None:
        given = jnp.concatenate([given, split_rows(sums)], 0)
    taken = lax.ppermute(given, "core", swap)
    total = (kept + taken[: 2 * rows].astype(jnp.float32)).astype(jnp.bfloat16)
    total = total.reshape(2, rows, 2, columns).transpose(2, 0, 1, 3)
    if sums is not None:
        sums = sums + join_rows(taken[2 * rows :], sums.shape[0])
        extra = split_rows(sums).reshape(16, 2, columns).transpose(1, 0, 2)
        total = jnp.concatenate([total, jnp.broadcast_to(extra[:, None], (2, 2, 16, columns))], 2)
    return total.reshape(4, total.shape[2], columns)


def body(
    activations,
    encoder,
    enc_bias,
    decoder,
    enc_moment,
    enc_second,
    bias_moment,
    bias_second,
    dec_moment,
    dec_second,
):
    rows_local, features = activations.shape
    total_rows = rows_local * 16
    depth, latents = encoder.shape
    enc_weights, dec_weights = gather_weights(encoder.astype(jnp.bfloat16), decoder.astype(jnp.bfloat16))
    piece = rows_local // 32
    planes = exchange(activations.reshape(16, 2 * piece, features), plane_axes)
    planes = planes.reshape(2, 2, 2, 2, 2, piece, features)
    planes = planes.transpose(4, 1, 2, 5, 0, 3, 6).reshape(8, piece, 4, features)
    own = exchange(planes, ("h", "zc", "zd")).reshape(2, 4, piece, 4, features)
    own = own.transpose(1, 2, 3, 0, 4).reshape(4 * piece, 8 * features)
    half = lax.axis_index("h")
    own, other_bias = lax.optimization_barrier((own, lax.ppermute(enc_bias, "h", swap)))
    bias = jnp.where(
        half == 0, jnp.concatenate([enc_bias, other_bias]), jnp.concatenate([other_bias, enc_bias])
    )
    acts = spread(own, plane_axes)
    rows = acts.shape[0]

    pre_part = jnp.dot(acts, enc_weights, preferred_element_type=jnp.float32)
    pre = add_blocks(pre_part.reshape(4, rows // 4, 2 * latents), depth_axes) + bias[None, :]
    codes = spread(jnp.maximum(pre, 0.0).astype(jnp.bfloat16), depth_axes)
    usage = jnp.sum(codes.astype(jnp.float32), axis=0)
    squares = jnp.sum(jnp.square(dec_weights.astype(jnp.float32)), axis=0)
    squares = total_over(squares, depth_axes[:1])

    recon_part = lax.dot_general(
        codes, dec_weights, (((1,), (1,)), ((), ())), preferred_element_type=jnp.float32
    ).astype(jnp.bfloat16)
    recon = add_blocks(recon_part.reshape(16, rows // 16, 4 * depth), plane_axes)
    recon, squares = lax.optimization_barrier((recon, squares))
    squares = total_over(squares, depth_axes[1:])
    error = spread((recon - own.astype(jnp.float32)).astype(jnp.bfloat16), plane_axes)
    error, squares = lax.optimization_barrier((error, squares))
    norms = jnp.sqrt(squares + norm_eps)

    back_part = jnp.dot(error, dec_weights, preferred_element_type=jnp.float32).astype(jnp.bfloat16)
    dcodes = (
        2.0 / total_rows * add_blocks(back_part.reshape(4, rows // 4, 2 * latents), depth_axes)
        + penalty / total_rows * norms[None, :]
    )
    data_part = (
        2.0
        / total_rows
        * lax.dot_general(error, codes, (((0,), (0,)), ((), ())), preferred_element_type=jnp.float32)
    )
    data_blocks = core_blocks(data_part, None, depth, latents)
    back = jnp.where(pre > 0.0, dcodes, 0.0).astype(jnp.bfloat16)
    back, data_blocks = lax.optimization_barrier((back, data_blocks))
    data_grad = add_blocks(data_blocks, row_axes)
    back = spread_depth(back)
    sums = jnp.stack([jnp.sum(back.astype(jnp.float32), axis=0), usage])

    enc_part = lax.dot_general(
        acts, back, (((0,), (0,)), ((), ())), preferred_element_type=jnp.float32
    )
    enc_blocks = exchange(core_blocks(enc_part, sums, depth, latents), row_axes)
    enc_grad = jnp.sum(enc_blocks[:, :depth].astype(jnp.float32), axis=0)
    sums = jnp.sum(join_rows(enc_blocks[:, depth:], sums.shape[0]), axis=0)

    bias_grad, usage = sums[0], sums[1]
    norms = jnp.where(half == 0, norms[:latents], norms[latents:])
    dec_grad = data_grad + penalty * (usage / total_rows)[None, :] * decoder / norms[None, :]
    enc_update = adam_update(enc_grad, enc_moment, enc_second)
    bias_update = adam_update(bias_grad, bias_moment, bias_second)
    dec_update = adam_update(dec_grad, dec_moment, dec_second)
    return (enc_update, bias_update, dec_update)


def solution(mesh):
    fine = Mesh(mesh.devices.reshape((2,) * 9), names)
    dp, latent = names[:4], names[4:]
    matrix, vector = P(dp, latent), P(latent)
    in_specs = (matrix, matrix, vector, matrix, matrix, matrix, vector, vector, matrix, matrix)
    out_specs = (matrix, vector, matrix)
    return jax.shard_map(body, mesh=fine, in_specs=in_specs, out_specs=out_specs, check_vma=False)
```

```python
import jax
import jax.numpy as jnp
from jax import lax
from jax.sharding import Mesh, PartitionSpec as P

penalty = 3.0
beta_one = 0.9
beta_two = 0.999
step_count = 10.0
tiny_eps = 1e-08
norm_eps = 1e-06

names = ("zb", "zc", "zd", "core", "y1", "y0", "x1", "x0", "h")
depth_axes = ("zc", "zd")
plane_axes = ("y1", "y0", "x1", "x0")
row_axes = ("h", "zb")
swap = ((0, 1), (1, 0))
cross = ((0, 3), (1, 2), (2, 1), (3, 0))


def exchange(values, axes):
    return lax.all_to_all(values, axes, 0, 0, tiled=True)


def spread(values, axes):
    count = 1
    for axis in axes:
        count *= lax.axis_size(axis)
    copies = jnp.broadcast_to(values[None], (count,) + values.shape)
    return exchange(copies, axes).reshape((count * values.shape[0],) + values.shape[1:])


def spread_depth(values):
    place = 2 * lax.axis_index("zc") + lax.axis_index("zd")
    whole = jnp.zeros((4,) + values.shape, values.dtype)
    parts = (
        values,
        lax.ppermute(values, "zd", swap),
        lax.ppermute(values, "zc", swap),
        lax.ppermute(values, depth_axes, cross),
    )
    for offset, part in enumerate(parts):
        whole = lax.dynamic_update_index_in_dim(whole, part, place ^ offset, 0)
    return whole.reshape((4 * values.shape[0],) + values.shape[1:])


def coded(values):
    power = jnp.square(jnp.square(jnp.square(values * 16.0)))
    return jnp.where(values < 0.0, -power, power).astype(jnp.bfloat16)


def decoded(codes):
    codes = codes.astype(jnp.float32)
    root = jnp.sqrt(jnp.sqrt(jnp.sqrt(jnp.abs(codes)))) * 0.0625
    return jnp.where(codes < 0.0, -root, root)


def total_over(values, axes):
    for axis in axes:
        values = values + lax.ppermute(values, axis, swap)
    return values


def add_blocks(values, axes):
    return jnp.sum(exchange(values, axes).astype(jnp.float32), axis=0)


def adam_update(grad, moment, second):
    first_new = beta_one * moment + (1.0 - beta_one) * grad
    second_new = beta_two * second + (1.0 - beta_two) * grad * grad
    first_hat = first_new / (1.0 - beta_one**step_count)
    second_hat = second_new / (1.0 - beta_two**step_count)
    return first_hat / (jnp.sqrt(second_hat) + tiny_eps)


def gather_weights(*blocks):
    count, (rows, columns) = len(blocks), blocks[0].shape
    parts = lax.all_gather(jnp.concatenate(blocks), row_axes + ("core",), axis=0, tiled=False)
    parts = parts.reshape(2, 4, count, rows, columns)
    parts = [[parts[half, :, index].reshape(4 * rows, columns) for half in range(2)] for index in range(count)]
    return [jnp.concatenate(halves, axis=1) for halves in parts]


def split_rows(values):
    high = values.astype(jnp.bfloat16)
    low = (values - high.astype(jnp.float32)).astype(jnp.bfloat16)
    padding = jnp.zeros((16 - 2 * values.shape[0],) + values.shape[1:], jnp.bfloat16)
    return jnp.concatenate([high, low, padding], 0)


def join_rows(rows, count):
    rows = rows.astype(jnp.float32)
    return rows[..., :count, :] + rows[..., count : 2 * count, :]


def core_blocks(grad, sums, rows, columns):
    core = lax.axis_index("core")
    grad = grad.reshape(2, 2, rows, 2 * columns)
    kept = lax.dynamic_index_in_dim(grad, core, 1, False).reshape(2 * rows, 2 * columns)
    given = lax.dynamic_index_in_dim(grad, 1 - core, 1, False).reshape(2 * rows, 2 * columns)
    given = given.astype(jnp.bfloat16)
    if sums is not None:
        given = jnp.concatenate([given, split_rows(sums)], 0)
    taken = lax.ppermute(given, "core", swap)
    total = (kept + taken[: 2 * rows].astype(jnp.float32)).astype(jnp.bfloat16)
    total = total.reshape(2, rows, 2, columns).transpose(2, 0, 1, 3)
    if sums is not None:
        sums = sums + join_rows(taken[2 * rows :], sums.shape[0])
        extra = split_rows(sums).reshape(16, 2, columns).transpose(1, 0, 2)
        total = jnp.concatenate([total, jnp.broadcast_to(extra[:, None], (2, 2, 16, columns))], 2)
    return total.reshape(4, total.shape[2], columns)


def body(
    activations,
    encoder,
    enc_bias,
    decoder,
    enc_moment,
    enc_second,
    bias_moment,
    bias_second,
    dec_moment,
    dec_second,
):
    rows_local, features = activations.shape
    total_rows = rows_local * 16
    depth, latents = encoder.shape
    enc_weights, dec_weights = gather_weights(encoder.astype(jnp.bfloat16), decoder.astype(jnp.bfloat16))
    piece = rows_local // 32
    planes = exchange(activations.reshape(16, 2 * piece, features), plane_axes)
    planes = planes.reshape(2, 2, 2, 2, 2, piece, features)
    planes = planes.transpose(4, 1, 2, 5, 0, 3, 6).reshape(8, piece, 4, features)
    own = exchange(planes, ("h", "zc", "zd")).reshape(2, 4, piece, 4, features)
    own = own.transpose(1, 2, 3, 0, 4).reshape(4 * piece, 8 * features)
    half = lax.axis_index("h")
    own, other_bias = lax.optimization_barrier((own, lax.ppermute(enc_bias, "h", swap)))
    bias = jnp.where(
        half == 0, jnp.concatenate([enc_bias, other_bias]), jnp.concatenate([other_bias, enc_bias])
    )
    acts = spread(own, plane_axes)
    rows = acts.shape[0]

    pre_part = jnp.dot(acts, enc_weights, preferred_element_type=jnp.float32)
    pre_part = exchange(coded(pre_part).reshape(4, rows // 4, 2 * latents), depth_axes)
    pre = jnp.sum(decoded(pre_part), axis=0) + bias[None, :]
    codes = spread(jnp.maximum(pre, 0.0).astype(jnp.bfloat16), depth_axes)
    usage = jnp.sum(codes.astype(jnp.float32), axis=0)
    squares = jnp.sum(jnp.square(dec_weights.astype(jnp.float32)), axis=0)
    squares = total_over(squares, depth_axes[:1])

    recon_part = lax.dot_general(
        codes, dec_weights, (((1,), (1,)), ((), ())), preferred_element_type=jnp.float32
    ).astype(jnp.bfloat16)
    recon = add_blocks(recon_part.reshape(16, rows // 16, 4 * depth), plane_axes)
    recon, squares = lax.optimization_barrier((recon, squares))
    squares = total_over(squares, depth_axes[1:])
    error = spread((recon - own.astype(jnp.float32)).astype(jnp.bfloat16), plane_axes)
    error, squares = lax.optimization_barrier((error, squares))
    norms = jnp.sqrt(squares + norm_eps)

    back_part = jnp.dot(error, dec_weights, preferred_element_type=jnp.float32).astype(jnp.bfloat16)
    dcodes = (
        2.0 / total_rows * add_blocks(back_part.reshape(4, rows // 4, 2 * latents), depth_axes)
        + penalty / total_rows * norms[None, :]
    )
    data_part = (
        2.0
        / total_rows
        * lax.dot_general(error, codes, (((0,), (0,)), ((), ())), preferred_element_type=jnp.float32)
    )
    data_blocks = core_blocks(data_part, None, depth, latents)
    back = jnp.where(pre > 0.0, dcodes, 0.0).astype(jnp.bfloat16)
    back, data_blocks = lax.optimization_barrier((back, data_blocks))
    data_grad = add_blocks(data_blocks, row_axes)
    back = spread_depth(back)
    sums = jnp.stack([jnp.sum(back.astype(jnp.float32), axis=0), usage])

    enc_part = lax.dot_general(
        acts, back, (((0,), (0,)), ((), ())), preferred_element_type=jnp.float32
    )
    enc_blocks = exchange(core_blocks(enc_part, sums, depth, latents), row_axes)
    enc_grad = jnp.sum(enc_blocks[:, :depth].astype(jnp.float32), axis=0)
    sums = jnp.sum(join_rows(enc_blocks[:, depth:], sums.shape[0]), axis=0)

    bias_grad, usage = sums[0], sums[1]
    norms = jnp.where(half == 0, norms[:latents], norms[latents:])
    dec_grad = data_grad + penalty * (usage / total_rows)[None, :] * decoder / norms[None, :]
    enc_update = adam_update(enc_grad, enc_moment, enc_second)
    bias_update = adam_update(bias_grad, bias_moment, bias_second)
    dec_update = adam_update(dec_grad, dec_moment, dec_second)
    return (enc_update, bias_update, dec_update)


def solution(mesh):
    fine = Mesh(mesh.devices.reshape((2,) * 9), names)
    dp, latent = names[:4], names[4:]
    matrix, vector = P(dp, latent), P(latent)
    in_specs = (matrix, matrix, vector, matrix, matrix, matrix, vector, vector, matrix, matrix)
    out_specs = (matrix, vector, matrix)
    return jax.shard_map(body, mesh=fine, in_specs=in_specs, out_specs=out_specs, check_vma=False)
```

```python
import jax
import jax.numpy as jnp
from jax import lax
from jax.sharding import Mesh, PartitionSpec as P

penalty = 3.0
beta_one = 0.9
beta_two = 0.999
step_count = 10.0
tiny_eps = 1e-08
norm_eps = 1e-06

names = ("zb", "zc", "zd", "core", "y1", "y0", "x1", "x0", "h")
depth_axes = ("zc", "zd")
plane_axes = ("y1", "y0", "x1", "x0")
row_axes = ("h", "zb")
swap = ((0, 1), (1, 0))
cross = ((0, 3), (1, 2), (2, 1), (3, 0))


def exchange(values, axes):
    return lax.all_to_all(values, axes, 0, 0, tiled=True)


def spread(values, axes):
    count = 1
    for axis in axes:
        count *= lax.axis_size(axis)
    copies = jnp.broadcast_to(values[None], (count,) + values.shape)
    return exchange(copies, axes).reshape((count * values.shape[0],) + values.shape[1:])


def spread_depth(values):
    for axis in ("zd", "zc"):
        place = lax.axis_index(axis)
        taken = lax.ppermute(values, axis, swap)
        values = jnp.concatenate([jnp.where(place == 0, values, taken), jnp.where(place == 0, taken, values)])
    return values


def coded(values):
    power = jnp.square(jnp.square(jnp.square(values * 16.0)))
    return jnp.where(values < 0.0, -power, power).astype(jnp.bfloat16)


def decoded(codes):
    codes = codes.astype(jnp.float32)
    root = jnp.sqrt(jnp.sqrt(jnp.sqrt(jnp.abs(codes)))) * 0.0625
    return jnp.where(codes < 0.0, -root, root)


def total_over(values, axes):
    for axis in axes:
        values = values + lax.ppermute(values, axis, swap)
    return values


def add_blocks(values, axes):
    return jnp.sum(exchange(values, axes).astype(jnp.float32), axis=0)


def adam_update(grad, moment, second):
    first_new = beta_one * moment + (1.0 - beta_one) * grad
    second_new = beta_two * second + (1.0 - beta_two) * grad * grad
    first_hat = first_new / (1.0 - beta_one**step_count)
    second_hat = second_new / (1.0 - beta_two**step_count)
    return first_hat / (jnp.sqrt(second_hat) + tiny_eps)


def gather_weights(*blocks):
    count, (rows, columns) = len(blocks), blocks[0].shape
    parts = lax.all_gather(jnp.concatenate(blocks), row_axes + ("core",), axis=0, tiled=False)
    parts = parts.reshape(2, 4, count, rows, columns)
    parts = [[parts[half, :, index].reshape(4 * rows, columns) for half in range(2)] for index in range(count)]
    return [jnp.concatenate(halves, axis=1) for halves in parts]


def split_rows(values):
    high = values.astype(jnp.bfloat16)
    low = (values - high.astype(jnp.float32)).astype(jnp.bfloat16)
    padding = jnp.zeros((16 - 2 * values.shape[0],) + values.shape[1:], jnp.bfloat16)
    return jnp.concatenate([high, low, padding], 0)


def join_rows(rows, count):
    rows = rows.astype(jnp.float32)
    return rows[..., :count, :] + rows[..., count : 2 * count, :]


def core_blocks(grad, sums, rows, columns):
    core = lax.axis_index("core")
    grad = grad.reshape(2, 2, rows, 2 * columns)
    kept = lax.dynamic_index_in_dim(grad, core, 1, False).reshape(2 * rows, 2 * columns)
    given = lax.dynamic_index_in_dim(grad, 1 - core, 1, False).reshape(2 * rows, 2 * columns)
    given = given.astype(jnp.bfloat16)
    if sums is not None:
        given = jnp.concatenate([given, split_rows(sums)], 0)
    taken = lax.ppermute(given, "core", swap)
    total = (kept + taken[: 2 * rows].astype(jnp.float32)).astype(jnp.bfloat16)
    total = total.reshape(2, rows, 2, columns).transpose(2, 0, 1, 3)
    if sums is not None:
        sums = sums + join_rows(taken[2 * rows :], sums.shape[0])
        extra = split_rows(sums).reshape(16, 2, columns).transpose(1, 0, 2)
        total = jnp.concatenate([total, jnp.broadcast_to(extra[:, None], (2, 2, 16, columns))], 2)
    return total.reshape(4, total.shape[2], columns)


def body(
    activations,
    encoder,
    enc_bias,
    decoder,
    enc_moment,
    enc_second,
    bias_moment,
    bias_second,
    dec_moment,
    dec_second,
):
    rows_local, features = activations.shape
    total_rows = rows_local * 16
    depth, latents = encoder.shape
    enc_weights, dec_weights = gather_weights(encoder.astype(jnp.bfloat16), decoder.astype(jnp.bfloat16))
    piece = rows_local // 32
    planes = exchange(activations.reshape(16, 2 * piece, features), plane_axes)
    planes = planes.reshape(2, 2, 2, 2, 2, piece, features)
    planes = planes.transpose(4, 1, 2, 5, 0, 3, 6).reshape(8, piece, 4, features)
    own = exchange(planes, ("h", "zc", "zd")).reshape(2, 4, piece, 4, features)
    own = own.transpose(1, 2, 3, 0, 4).reshape(4 * piece, 8 * features)
    half = lax.axis_index("h")
    own, other_bias = lax.optimization_barrier((own, lax.ppermute(enc_bias, "h", swap)))
    bias = jnp.where(
        half == 0, jnp.concatenate([enc_bias, other_bias]), jnp.concatenate([other_bias, enc_bias])
    )
    acts = spread(own, plane_axes)
    rows = acts.shape[0]

    pre_part = jnp.dot(acts, enc_weights, preferred_element_type=jnp.float32)
    pre_part = exchange(coded(pre_part).reshape(4, rows // 4, 2 * latents), depth_axes)
    pre = jnp.sum(decoded(pre_part), axis=0) + bias[None, :]
    codes = spread(jnp.maximum(pre, 0.0).astype(jnp.bfloat16), depth_axes)
    usage = jnp.sum(codes.astype(jnp.float32), axis=0)
    squares = jnp.sum(jnp.square(dec_weights.astype(jnp.float32)), axis=0)
    squares = total_over(squares, depth_axes[:1])

    recon_part = lax.dot_general(
        codes, dec_weights, (((1,), (1,)), ((), ())), preferred_element_type=jnp.float32
    ).astype(jnp.bfloat16)
    recon = add_blocks(recon_part.reshape(16, rows // 16, 4 * depth), plane_axes)
    recon, squares = lax.optimization_barrier((recon, squares))
    squares = total_over(squares, depth_axes[1:])
    error = spread((recon - own.astype(jnp.float32)).astype(jnp.bfloat16), plane_axes)
    error, squares = lax.optimization_barrier((error, squares))
    norms = jnp.sqrt(squares + norm_eps)

    back_part = jnp.dot(error, dec_weights, preferred_element_type=jnp.float32).astype(jnp.bfloat16)
    dcodes = (
        2.0 / total_rows * add_blocks(back_part.reshape(4, rows // 4, 2 * latents), depth_axes)
        + penalty / total_rows * norms[None, :]
    )
    data_part = (
        2.0
        / total_rows
        * lax.dot_general(error, codes, (((0,), (0,)), ((), ())), preferred_element_type=jnp.float32)
    )
    data_blocks = core_blocks(data_part, None, depth, latents)
    back = jnp.where(pre > 0.0, dcodes, 0.0).astype(jnp.bfloat16)
    back, data_blocks = lax.optimization_barrier((back, data_blocks))
    data_grad = add_blocks(data_blocks, row_axes)
    back = spread_depth(back)
    sums = jnp.stack([jnp.sum(back.astype(jnp.float32), axis=0), usage])

    enc_part = lax.dot_general(
        acts, back, (((0,), (0,)), ((), ())), preferred_element_type=jnp.float32
    )
    enc_blocks = exchange(core_blocks(enc_part, sums, depth, latents), row_axes)
    enc_grad = jnp.sum(enc_blocks[:, :depth].astype(jnp.float32), axis=0)
    sums = jnp.sum(join_rows(enc_blocks[:, depth:], sums.shape[0]), axis=0)

    bias_grad, usage = sums[0], sums[1]
    norms = jnp.where(half == 0, norms[:latents], norms[latents:])
    dec_grad = data_grad + penalty * (usage / total_rows)[None, :] * decoder / norms[None, :]
    enc_update = adam_update(enc_grad, enc_moment, enc_second)
    bias_update = adam_update(bias_grad, bias_moment, bias_second)
    dec_update = adam_update(dec_grad, dec_moment, dec_second)
    return (enc_update, bias_update, dec_update)


def solution(mesh):
    fine = Mesh(mesh.devices.reshape((2,) * 9), names)
    dp, latent = names[:4], names[4:]
    matrix, vector = P(dp, latent), P(latent)
    in_specs = (matrix, matrix, vector, matrix, matrix, matrix, vector, vector, matrix, matrix)
    out_specs = (matrix, vector, matrix)
    return jax.shard_map(body, mesh=fine, in_specs=in_specs, out_specs=out_specs, check_vma=False)
```

```python
import jax
import jax.numpy as jnp
from jax import lax
from jax.sharding import Mesh, PartitionSpec as P

penalty = 3.0
beta_one = 0.9
beta_two = 0.999
step_count = 10.0
tiny_eps = 1e-08
norm_eps = 1e-06

names = ("zb", "zc", "zd", "core", "y1", "y0", "x1", "x0", "h")
depth_axes = ("zc", "zd")
plane_axes = ("y1", "y0", "x1", "x0")
row_axes = ("h", "zb")
swap = ((0, 1), (1, 0))
cross = ((0, 3), (1, 2), (2, 1), (3, 0))


def exchange(values, axes):
    return lax.all_to_all(values, axes, 0, 0, tiled=True)


def spread(values, axes):
    count = 1
    for axis in axes:
        count *= lax.axis_size(axis)
    copies = jnp.broadcast_to(values[None], (count,) + values.shape)
    return exchange(copies, axes).reshape((count * values.shape[0],) + values.shape[1:])


def spread_depth(values):
    place = 2 * lax.axis_index("zc") + lax.axis_index("zd")
    whole = jnp.zeros((4,) + values.shape, values.dtype)
    parts = (
        values,
        lax.ppermute(values, "zd", swap),
        lax.ppermute(values, "zc", swap),
        lax.ppermute(values, depth_axes, cross),
    )
    for offset, part in enumerate(parts):
        whole = lax.dynamic_update_index_in_dim(whole, part, place ^ offset, 0)
    return whole.reshape((4 * values.shape[0],) + values.shape[1:])


def coded(values):
    power = jnp.square(jnp.square(jnp.square(values * 16.0)))
    return jnp.where(values < 0.0, -power, power).astype(jnp.bfloat16)


def decoded(codes):
    codes = codes.astype(jnp.float32)
    root = jnp.sqrt(jnp.sqrt(jnp.sqrt(jnp.abs(codes)))) * 0.0625
    return jnp.where(codes < 0.0, -root, root)


def total_over(values, axes):
    for axis in axes:
        values = values + lax.ppermute(values, axis, swap)
    return values


def add_blocks(values, axes):
    return jnp.sum(exchange(values, axes).astype(jnp.float32), axis=0)


def adam_update(grad, moment, second):
    first_new = beta_one * moment + (1.0 - beta_one) * grad
    second_new = beta_two * second + (1.0 - beta_two) * grad * grad
    first_hat = first_new / (1.0 - beta_one**step_count)
    second_hat = second_new / (1.0 - beta_two**step_count)
    return first_hat / (jnp.sqrt(second_hat) + tiny_eps)


def gather_weights(*blocks):
    count, (rows, columns) = len(blocks), blocks[0].shape
    parts = lax.all_gather(jnp.concatenate(blocks), row_axes + ("core",), axis=0, tiled=False)
    parts = parts.reshape(2, 4, count, rows, columns)
    parts = [[parts[half, :, index].reshape(4 * rows, columns) for half in range(2)] for index in range(count)]
    return [jnp.concatenate(halves, axis=1) for halves in parts]


def split_rows(values):
    high = values.astype(jnp.bfloat16)
    low = (values - high.astype(jnp.float32)).astype(jnp.bfloat16)
    padding = jnp.zeros((16 - 2 * values.shape[0],) + values.shape[1:], jnp.bfloat16)
    return jnp.concatenate([high, low, padding], 0)


def join_rows(rows, count):
    rows = rows.astype(jnp.float32)
    return rows[..., :count, :] + rows[..., count : 2 * count, :]


def core_blocks(grad, sums, rows, columns):
    core = lax.axis_index("core")
    grad = grad.reshape(2, 2, rows, 2 * columns)
    kept = lax.dynamic_index_in_dim(grad, core, 1, False).reshape(2 * rows, 2 * columns)
    given = lax.dynamic_index_in_dim(grad, 1 - core, 1, False).reshape(2 * rows, 2 * columns)
    given = given.astype(jnp.bfloat16)
    if sums is not None:
        given = jnp.concatenate([given, split_rows(sums)], 0)
    taken = lax.ppermute(given, "core", swap)
    total = (kept + taken[: 2 * rows].astype(jnp.float32)).astype(jnp.bfloat16)
    total = total.reshape(2, rows, 2, columns).transpose(2, 0, 1, 3)
    if sums is not None:
        sums = sums + join_rows(taken[2 * rows :], sums.shape[0])
        extra = split_rows(sums).reshape(16, 2, columns).transpose(1, 0, 2)
        total = jnp.concatenate([total, jnp.broadcast_to(extra[:, None], (2, 2, 16, columns))], 2)
    return total.reshape(4, total.shape[2], columns)


def body(
    activations,
    encoder,
    enc_bias,
    decoder,
    enc_moment,
    enc_second,
    bias_moment,
    bias_second,
    dec_moment,
    dec_second,
):
    rows_local, features = activations.shape
    total_rows = rows_local * 16
    depth, latents = encoder.shape
    enc_weights, dec_weights = gather_weights(encoder.astype(jnp.bfloat16), decoder.astype(jnp.bfloat16))
    piece = rows_local // 32
    planes = exchange(activations.reshape(16, 2 * piece, features), plane_axes)
    planes = planes.reshape(2, 2, 2, 2, 2, piece, features)
    planes = planes.transpose(4, 1, 2, 5, 0, 3, 6).reshape(8, piece, 4 * features)
    own = exchange(planes, ("h", "zc", "zd")).reshape(2, 4, piece, 4, features)
    own = own.transpose(1, 2, 3, 0, 4).reshape(4 * piece, 8 * features)
    half = lax.axis_index("h")
    own, other_bias = lax.optimization_barrier((own, lax.ppermute(enc_bias, "h", swap)))
    bias = jnp.where(
        half == 0, jnp.concatenate([enc_bias, other_bias]), jnp.concatenate([other_bias, enc_bias])
    )
    acts = spread(own, plane_axes)
    rows = acts.shape[0]

    pre_part = jnp.dot(acts, enc_weights, preferred_element_type=jnp.float32)
    pre_part = exchange(coded(pre_part).reshape(4, rows // 4, 2 * latents), depth_axes)
    pre = jnp.sum(decoded(pre_part), axis=0) + bias[None, :]
    codes = spread(jnp.maximum(pre, 0.0).astype(jnp.bfloat16), depth_axes)
    usage = jnp.sum(codes.astype(jnp.float32), axis=0)
    squares = jnp.sum(jnp.square(dec_weights.astype(jnp.float32)), axis=0)
    squares = total_over(squares, depth_axes[:1])

    recon_part = lax.dot_general(
        codes, dec_weights, (((1,), (1,)), ((), ())), preferred_element_type=jnp.float32
    ).astype(jnp.bfloat16)
    recon = add_blocks(recon_part.reshape(16, rows // 16, 4 * depth), plane_axes)
    recon, squares = lax.optimization_barrier((recon, squares))
    squares = total_over(squares, depth_axes[1:])
    error = spread((recon - own.astype(jnp.float32)).astype(jnp.bfloat16), plane_axes)
    error, squares = lax.optimization_barrier((error, squares))
    norms = jnp.sqrt(squares + norm_eps)

    back_part = jnp.dot(error, dec_weights, preferred_element_type=jnp.float32).astype(jnp.bfloat16)
    dcodes = (
        2.0 / total_rows * add_blocks(back_part.reshape(4, rows // 4, 2 * latents), depth_axes)
        + penalty / total_rows * norms[None, :]
    )
    data_part = (
        2.0
        / total_rows
        * lax.dot_general(error, codes, (((0,), (0,)), ((), ())), preferred_element_type=jnp.float32)
    )
    data_blocks = core_blocks(data_part, None, depth, latents)
    back = jnp.where(pre > 0.0, dcodes, 0.0).astype(jnp.bfloat16)
    back, data_blocks = lax.optimization_barrier((back, data_blocks))
    data_grad = add_blocks(data_blocks, row_axes)
    back = spread_depth(back)
    sums = jnp.stack([jnp.sum(back.astype(jnp.float32), axis=0), usage])

    enc_part = lax.dot_general(
        acts, back, (((0,), (0,)), ((), ())), preferred_element_type=jnp.float32
    )
    enc_blocks = exchange(core_blocks(enc_part, sums, depth, latents), row_axes)
    enc_grad = jnp.sum(enc_blocks[:, :depth].astype(jnp.float32), axis=0)
    sums = jnp.sum(join_rows(enc_blocks[:, depth:], sums.shape[0]), axis=0)

    bias_grad, usage = sums[0], sums[1]
    norms = jnp.where(half == 0, norms[:latents], norms[latents:])
    dec_grad = data_grad + penalty * (usage / total_rows)[None, :] * decoder / norms[None, :]
    enc_update = adam_update(enc_grad, enc_moment, enc_second)
    bias_update = adam_update(bias_grad, bias_moment, bias_second)
    dec_update = adam_update(dec_grad, dec_moment, dec_second)
    return (enc_update, bias_update, dec_update)


def solution(mesh):
    fine = Mesh(mesh.devices.reshape((2,) * 9), names)
    dp, latent = names[:4], names[4:]
    matrix, vector = P(dp, latent), P(latent)
    in_specs = (matrix, matrix, vector, matrix, matrix, matrix, vector, vector, matrix, matrix)
    out_specs = (matrix, vector, matrix)
    return jax.shard_map(body, mesh=fine, in_specs=in_specs, out_specs=out_specs, check_vma=False)
```
